32 devices in a mesh: group: 2 (over x), tile: 16 (over z, y, core).
Axes of the slice: x: 2, y: 2, z: 4, core: 2. Of those that a mesh axis runs over, the one named last changes fastest.
Arguments:
- samples: bfloat16 [2, 1024, 65984], P(None, ('group', 'tile')), parts along dimension 1, may hold values from -6 to 6
- fir_taps: float32 [8, 64], replicated, may hold values from -2 to 2
- chan_map: int32 [32], replicated, may hold values from 0 to 63, as said below
- layout: int32 [10], replicated, may hold values from 0 to 9, each once
Outputs:
- visibilities: float32 [640, 2, 128, 128], P(('group', 'tile')), parts along dimension 0
The draws below stay inside these ranges and needn't reach their ends.
There are 2 independent parts, one for each index of `group`. The reference program is written for one: setup_inputs(seed, part) draws one part's arguments, and reference() takes and returns one part's arrays. A program takes and returns all parts, laid end to end along the dimension named above; an argument that names none is the same for every part. Nothing has to cross between parts.
Inputs may be any that keep to these rules, and one draw needn't show every extreme that they name: `chan_map`: 32 distinct channels in increasing order; channels 0 and 63 are always kept. `layout`: each block pair once.
All inputs are finite; a program needn't handle non-finite values.
Results may differ from the reference program's by a relative error of at most 0.0033.
Values may be sent and summed in bfloat16 or wider, within the bound.
A program may use at most 128 MiB of HBM per device.

```python
import math
import jax
import jax.numpy as jnp
import numpy as np
from jax import lax

NIN = 512
NCHAN = 64
KEEP = 32
TAPS = 8
BLOCK = 128
SPEC = 1024
SAMPLES = 65984
NBLK = 4
NPAIR = 10


def draw_chan_map(key, part):
    interior = jax.random.permutation(key, NCHAN - 2)[:KEEP - 2] + 1
    band_edges = jnp.array([0, NCHAN - 1], dtype=jnp.int32)
    picked = jnp.concatenate([band_edges, interior.astype(jnp.int32)])
    return jnp.sort(picked).astype(jnp.int32)


def block_levels(stream_key, dims, split, low, top_value):
    level = 1.0
    for axis_at, shards_of in split:
        draws = jax.random.uniform(jax.random.fold_in(jax.random.fold_in(stream_key, 6), axis_at), (shards_of,), jnp.float32, low / len(split), top_value / len(split))
        level = level * jnp.repeat(jnp.exp(draws), dims[axis_at] // shards_of).reshape((-1,) + (1,) * (len(dims) - 1 - axis_at))
    return level


def noise(own_key, dims, spread, most, cuts=(), held_as=jnp.bfloat16):
    values = jax.random.normal(own_key, dims, jnp.float32) * spread
    if len(cuts) > 0:
        values = block_levels(own_key, dims, cuts, -0.22, 0.18) * values
    return jnp.clip(values, min=-most, max=most).astype(held_as)


def setup_inputs(seed: int = 0, part: int = 0) -> dict:
    splits = jax.random.split(jax.random.key(seed), 5)
    part_keys = jax.random.split(jax.random.fold_in(splits[4], part), 5)
    return {
        "samples": noise(part_keys[0], (2, NIN, SAMPLES), 1.0, 6.0, ((1, 16),)),
        "fir_taps": noise(splits[1], (TAPS, NCHAN), TAPS ** -0.5, 2.0, (), jnp.float32),
        "chan_map": draw_chan_map(jax.random.fold_in(splits[4], 71), part),
        "layout": jax.random.permutation(splits[3], NPAIR).astype(jnp.int32),
    }


def pair_tables(block_count):
    first_block = []
    second_block = []
    for i in range(block_count):
        for j in range(i, block_count):
            first_block.append(i)
            second_block.append(j)
    return (np.array(first_block, np.int32), np.array(second_block, np.int32))

def dft_table(chan_map):
    tap_index = jnp.arange(NCHAN, dtype=jnp.int32)
    phases = tap_index[:, None] * chan_map[None, :] % NCHAN
    angles = phases.astype(jnp.float32) * (2.0 * math.pi / NCHAN)
    scaling = 1.0 / math.sqrt(NCHAN)
    cosine = jnp.cos(angles) * scaling
    sine_part = jnp.sin(angles) * scaling
    real_rows = jnp.stack([cosine, -sine_part], 1)
    imag_rows = jnp.stack([sine_part, cosine], 1)
    return jnp.stack([real_rows, imag_rows], 0).astype(jnp.bfloat16)

def weigh(sample_block, fir_taps):
    summed = jnp.zeros(sample_block.shape[:2] + (SPEC * NCHAN,), jnp.float32)
    for k in range(TAPS):
        window = lax.slice_in_dim(sample_block, k * NCHAN, k * NCHAN + SPEC * NCHAN, axis=2).astype(jnp.float32)
        summed = summed + window * jnp.tile(fir_taps[k], SPEC)
    return summed.astype(jnp.bfloat16)

def reference(samples, fir_taps, chan_map, layout):
    dft_rows = dft_table(chan_map).astype(jnp.float32)
    group_size = min(NIN, 8)
    group_total = NIN // group_size

    def spectra_of(group_index):
        start = (group_index * group_size).astype(jnp.int32)
        sample_block = lax.dynamic_slice_in_dim(samples, start, group_size, 1)
        weighted = weigh(sample_block, fir_taps).reshape(2, group_size, SPEC, NCHAN)
        spectra = jnp.einsum('rnqc,ritn->iqct', dft_rows, weighted.astype(jnp.float32), precision=lax.Precision.HIGHEST)
        return spectra.astype(jnp.bfloat16)
    spectra_all = lax.map(spectra_of, jnp.arange(group_total, dtype=jnp.int32))
    spectra_all = spectra_all.reshape(NIN, 2, KEEP, SPEC)
    first_block, second_block = pair_tables(NBLK)
    first_sel = jnp.asarray(first_block)[layout]
    second_sel = jnp.asarray(second_block)[layout]

    def correlate(channel):
        single = lax.dynamic_index_in_dim(spectra_all, channel, 2, keepdims=False)
        blocks = single.reshape(NBLK, BLOCK, 2, SPEC).astype(jnp.float32)
        left_side = blocks[first_sel]
        right_side = blocks[second_sel]
        swapped = jnp.stack([-right_side[:, :, 1], right_side[:, :, 0]], 2)
        real_part = jnp.einsum('kapt,kbpt->kab', left_side, right_side, precision=lax.Precision.HIGHEST)
        imag_part = jnp.einsum('kapt,kbpt->kab', left_side, swapped, precision=lax.Precision.HIGHEST)
        return jnp.stack([real_part, imag_part], 1) / SPEC
    result = lax.map(correlate, jnp.arange(KEEP, dtype=jnp.int32))
    return result.reshape(KEEP * NPAIR, 2, BLOCK, BLOCK)
```

```python
import functools
import math

import jax
import jax.numpy as jnp
import numpy as np
from jax import lax
from jax.experimental import pallas as pl
from jax.experimental.pallas import tpu as pltpu
from jax.sharding import PartitionSpec as P

NCHAN = 64
KEEP = 32
TAPS = 8
BLOCK = 128
NBLK = 4
NPAIR = 10

DT = 8
STRIDE = DT * NCHAN
TAIL = (TAPS - 1) * NCHAN
WIDE = 2 * STRIDE
LANES = 128
MESH = pl.DeviceIdType.MESH
NT = (((1,), (1,)), ((), ()))


def pair_tables(block_count):
    pairs = [(i, j) for i in range(block_count) for j in range(i, block_count)]
    return tuple(np.array(side, np.int32) for side in zip(*pairs))


def dft_table(channels):
    tap_index = jnp.arange(NCHAN, dtype=jnp.int32)
    angles = (tap_index[:, None] * channels[None] % NCHAN).astype(jnp.float32) * (
        2.0 * math.pi / NCHAN
    )
    scaling = 1.0 / math.sqrt(NCHAN)
    cosine = jnp.cos(angles) * scaling
    sine_part = jnp.sin(angles) * scaling
    real_rows = jnp.stack([cosine, -sine_part], 1)
    imag_rows = jnp.stack([sine_part, cosine], 1)
    return jnp.stack([real_rows, imag_rows], 0).astype(jnp.bfloat16)


def partner(me, k, bits):
    return sum(
        ((me // (1 << b) + (k >> b & 1)) % 2) * (1 << b) for b in range(bits)
    )


def kernel(
    tiles,
    chunks,
    layout_ref,
    dft_ref,
    fir_ref,
    samples_ref,
    out_ref,
    held,
    filt,
    window,
    send,
    recv,
    left,
    right,
    total,
    load_sem,
    own_sem,
    send_sem,
    recv_sem,
):
    bits = tiles.bit_length() - 1
    me = lax.axis_index("tile")
    per = 16 * STRIDE
    inputs = samples_ref.shape[1]
    order = sorted(range(1, tiles), reverse=True)
    chans = KEEP // tiles

    def load(c):
        at = pl.ds(pl.multiple_of(c * per, per), per)
        return pltpu.make_async_copy(
            samples_ref.at[:, :, at], held.at[:, :, at], load_sem.at[c]
        )

    rest = pltpu.make_async_copy(
        samples_ref.at[:, :, pl.ds(chunks * per, TAIL)],
        held.at[:, :, pl.ds(chunks * per, TAIL)],
        load_sem.at[chunks],
    )
    for c in range(chunks):
        load(c).start()
    rest.start()

    barrier = pltpu.get_barrier_semaphore()
    for k in order:
        pl.semaphore_signal(
            barrier, inc=1, device_id={"tile": partner(me, k, bits)}, device_id_type=MESH
        )

    def out_copy(c, k):
        there = partner(me, k, bits)
        return pltpu.make_async_remote_copy(
            src_ref=send.at[c, there],
            dst_ref=recv.at[c, me],
            send_sem=send_sem.at[c, k],
            recv_sem=recv_sem.at[c, k],
            device_id={"tile": there},
            device_id_type=MESH,
        )

    def own_copy(c):
        return pltpu.make_async_copy(send.at[c, me], recv.at[c, me], own_sem.at[c])

    for r in range(2):
        for b in range(WIDE // LANES):
            taps = fir_ref[:, b * LANES : (b + 1) * LANES]
            both = dft_ref[r][:, None, :] * taps[None]
            filt[:, r * WIDE + b * LANES : r * WIDE + (b + 1) * LANES] = both.reshape(
                KEEP * 2 * DT, LANES
            ).astype(jnp.bfloat16)
    window[...] = jnp.zeros_like(window)
    pl.semaphore_wait(barrier, tiles - 1)
    load(0).wait()

    def channelize(c, carry):
        @pl.when(c + 1 < chunks)
        def _():
            load(c + 1).wait()

        @pl.when(c + 1 == chunks)
        def _():
            rest.wait()

        parts = []
        for f in range(2):
            for r in range(2):
                for q in range(8):
                    at = (c * 16 + f * 8 + q) * STRIDE
                    rows = slice(q * inputs, (q + 1) * inputs)
                    window[rows, r * WIDE : r * WIDE + STRIDE] = held[
                        r, :, pl.ds(pl.multiple_of(at, STRIDE), STRIDE)
                    ]
                    window[rows, r * WIDE + STRIDE : r * WIDE + STRIDE + TAIL] = held[
                        r, :, pl.ds(pl.multiple_of(at + STRIDE, STRIDE), TAIL)
                    ]
            got = lax.dot_general(
                filt[...], window[...], NT, preferred_element_type=jnp.float32
            )
            for h in range(2):
                parts.append(
                    got[:, h * LANES : (h + 1) * LANES].reshape(KEEP * 2, DT, LANES)
                )
        block = jnp.concatenate(parts, axis=1).astype(jnp.bfloat16)
        send[c] = block.reshape(tiles, chans * 2, 4 * DT, LANES)
        for k in order:
            out_copy(c, k).start()
        own_copy(c).start()
        return carry

    lax.fori_loop(0, chunks, channelize, 0)
    total[...] = jnp.zeros_like(total)

    def correlate(x, carry):
        for half in range(2):
            for k in order:
                out_copy(2 * x + half, k).wait_recv()
            own_copy(2 * x + half).wait()

        def turn(src, inner):
            rows = 4 * DT * 2
            for ch in range(chans):
                sides = []
                for p in range(2):
                    for half in range(2):
                        sides.append(recv[2 * x + half, src, ch * 2 + p])
                re0, re1, im0, im1 = sides
                one = jnp.concatenate([re0, re1, im0, im1], axis=0).T
                two = jnp.concatenate([-im0, -im1, re0, re1], axis=0).T
                place = pl.ds(pl.multiple_of(src * inputs, inputs), inputs)
                for g in range(LANES // inputs):
                    at = slice(g * 2 * rows, (g + 1) * 2 * rows)
                    left[ch, place, at] = one[g * inputs : (g + 1) * inputs]
                    right[ch, place, at] = two[g * inputs : (g + 1) * inputs]
            return inner

        lax.fori_loop(0, tiles, turn, 0)
        for ch in range(chans):
            for j in range(NBLK):
                cols = slice(j * BLOCK, (j + 1) * BLOCK)
                rhs = jnp.concatenate([left[ch, cols, :], right[ch, cols, :]], axis=0)
                got = lax.dot_general(
                    left[ch, : (j + 1) * BLOCK, :],
                    rhs,
                    NT,
                    preferred_element_type=jnp.float32,
                )
                for i in range(j + 1):
                    q = ch * NPAIR + i * NBLK - i * (i - 1) // 2 + j - i
                    for p in range(2):
                        total[q, p] += got[
                            i * BLOCK : (i + 1) * BLOCK, p * BLOCK : (p + 1) * BLOCK
                        ]
        return carry

    lax.fori_loop(0, chunks // 2, correlate, 0)

    scale = 1.0 / (chunks * 16 * DT)
    for p in range(NPAIR):
        q = layout_ref[p]
        for ch in range(chans):
            out_ref[ch * NPAIR + p] = total[ch * NPAIR + q] * scale

    def drain(c, carry):
        for k in order:
            out_copy(c, k).wait_send()
        return carry

    lax.fori_loop(0, chunks, drain, 0)


def fused(samples, fir_taps, chan_map, layout):
    tiles = lax.axis_size("tile")
    inputs = samples.shape[1]
    spec_count = samples.shape[2] // NCHAN - TAPS + 1
    chunks = spec_count // (16 * DT)
    chans = KEEP // tiles
    table = dft_table(chan_map).astype(jnp.float32)
    table = table.transpose(0, 3, 2, 1).reshape(2, KEEP * 2, NCHAN)
    table = jnp.concatenate([table, table], axis=2)
    fir = jnp.stack(
        [jnp.pad(fir_taps, ((dt, DT - dt), (0, 0))).reshape(WIDE) for dt in range(DT)]
    )
    half = 4 * DT
    blocks = (chunks, tiles, chans * 2, half, LANES)
    turned = (chans, tiles * inputs, 4 * half * LANES // inputs)
    result = (chans * NPAIR, 2, BLOCK, BLOCK)
    vmem = pl.BlockSpec(memory_space=pltpu.VMEM)
    return pl.pallas_call(
        functools.partial(kernel, tiles, chunks),
        out_shape=jax.ShapeDtypeStruct(result, jnp.float32),
        in_specs=[
            pl.BlockSpec(memory_space=pltpu.SMEM),
            vmem,
            vmem,
            pl.BlockSpec(memory_space=pl.ANY),
        ],
        out_specs=vmem,
        scratch_shapes=[
            pltpu.VMEM(samples.shape, jnp.bfloat16),
            pltpu.VMEM((KEEP * 2 * DT, 2 * WIDE), jnp.bfloat16),
            pltpu.VMEM((8 * inputs, 2 * WIDE), jnp.bfloat16),
            pltpu.VMEM(blocks, jnp.bfloat16),
            pltpu.VMEM(blocks, jnp.bfloat16),
            pltpu.VMEM(turned, jnp.bfloat16),
            pltpu.VMEM(turned, jnp.bfloat16),
            pltpu.VMEM(result, jnp.float32),
            pltpu.SemaphoreType.DMA((chunks + 1,)),
            pltpu.SemaphoreType.DMA((chunks,)),
            pltpu.SemaphoreType.DMA((chunks, tiles)),
            pltpu.SemaphoreType.DMA((chunks, tiles)),
        ],
        compiler_params=pltpu.CompilerParams(
            collective_id=0,
            has_side_effects=True,
            vmem_limit_bytes=48 * 1024 * 1024,
        ),
    )(layout, table, fir, samples)


def plain(samples, fir_taps, chan_map, layout):
    tiles = lax.axis_size("tile")
    inputs = samples.shape[1]
    spec_count = samples.shape[2] // NCHAN - TAPS + 1
    summed = jnp.zeros((2, inputs, spec_count * NCHAN), jnp.float32)
    for k in range(TAPS):
        part = lax.slice_in_dim(samples, k * NCHAN, (k + spec_count) * NCHAN, axis=2)
        summed = summed + part.astype(jnp.float32) * jnp.tile(fir_taps[k], spec_count)
    weighted = summed.astype(jnp.bfloat16).reshape(2, inputs, spec_count, NCHAN)
    spectra = jnp.einsum(
        "rnqc,ritn->ciqt", dft_table(chan_map), weighted, preferred_element_type=jnp.float32
    ).astype(jnp.bfloat16)
    rows = KEEP * NPAIR // tiles
    held = max(1, rows // NPAIR)
    spectra = jnp.repeat(spectra, max(1, NPAIR // rows), axis=0)
    spectra = spectra.reshape(tiles, held, inputs, 2, spec_count)
    got = lax.all_to_all(spectra, "tile", split_axis=0, concat_axis=2, tiled=True)
    got = got.reshape(held, tiles * inputs, 2, spec_count)
    swapped = jnp.stack([-got[:, :, 1], got[:, :, 0]], 2)
    first, second = pair_tables(NBLK)
    kinds = [
        jnp.einsum("capt,cbpt->cab", got, side, preferred_element_type=jnp.float32)
        for side in (got, swapped)
    ]
    blocks = jnp.stack(
        [
            jnp.stack(
                [
                    kind[:, i * BLOCK : (i + 1) * BLOCK, j * BLOCK : (j + 1) * BLOCK]
                    for kind in kinds
                ],
                1,
            )
            for i, j in zip(first, second)
        ],
        1,
    )
    start = lax.axis_index("tile") * rows % NPAIR
    out = []
    for row in range(rows):
        spot = (start + row) % NPAIR
        pair = jnp.sum(jnp.where(jnp.arange(NPAIR) == spot, layout, 0))
        chosen = (jnp.arange(NPAIR) == pair)[:, None, None, None]
        out.append(jnp.sum(jnp.where(chosen, blocks[row // NPAIR], 0.0), 0))
    return jnp.stack(out) / spec_count


def on_device(samples, fir_taps, chan_map, layout):
    tiles = lax.axis_size("tile")
    inputs = samples.shape[1]
    spec_count = samples.shape[2] // NCHAN - TAPS + 1
    fits = tiles == 16 and inputs == 32 and spec_count % (32 * DT) == 0
    return (fused if fits and spec_count <= 1024 else plain)(
        samples, fir_taps, chan_map, layout
    )


def solution(mesh):
    placed = (P(None, ("group", "tile"), None), P(), P(), P())
    return jax.shard_map(
        on_device,
        mesh=mesh,
        in_specs=placed,
        out_specs=P(("group", "tile"), None, None, None),
        check_vma=False,
    )
```

```python
import functools
import math

import jax
import jax.numpy as jnp
import numpy as np
from jax import lax
from jax.experimental import pallas as pl
from jax.experimental.pallas import tpu as pltpu
from jax.sharding import PartitionSpec as P

NCHAN = 64
KEEP = 32
TAPS = 8
BLOCK = 128
NBLK = 4
NPAIR = 10

DT = 8
STRIDE = DT * NCHAN
TAIL = (TAPS - 1) * NCHAN
WIDE = 2 * STRIDE
LANES = 128
MESH = pl.DeviceIdType.MESH
NT = (((1,), (1,)), ((), ()))


def pair_tables(block_count):
    pairs = [(i, j) for i in range(block_count) for j in range(i, block_count)]
    return tuple(np.array(side, np.int32) for side in zip(*pairs))


def dft_table(channels):
    tap_index = jnp.arange(NCHAN, dtype=jnp.int32)
    angles = (tap_index[:, None] * channels[None] % NCHAN).astype(jnp.float32) * (
        2.0 * math.pi / NCHAN
    )
    scaling = 1.0 / math.sqrt(NCHAN)
    cosine = jnp.cos(angles) * scaling
    sine_part = jnp.sin(angles) * scaling
    real_rows = jnp.stack([cosine, -sine_part], 1)
    imag_rows = jnp.stack([sine_part, cosine], 1)
    return jnp.stack([real_rows, imag_rows], 0).astype(jnp.bfloat16)


def partner(me, k, bits):
    return sum(
        ((me // (1 << b) + (k >> b & 1)) % 2) * (1 << b) for b in range(bits)
    )


def kernel(
    tiles,
    chunks,
    layout_ref,
    chan_ref,
    fir_ref,
    samples_ref,
    out_ref,
    held,
    spread,
    filt,
    window,
    send,
    recv,
    left,
    right,
    total,
    load_sem,
    own_sem,
    send_sem,
    recv_sem,
):
    bits = tiles.bit_length() - 1
    me = lax.axis_index("tile")
    per = 16 * STRIDE
    inputs = samples_ref.shape[1]
    order = list(range(1, tiles))
    chans = KEEP // tiles

    def load(c):
        at = pl.ds(pl.multiple_of(c * per, per), per)
        return pltpu.make_async_copy(
            samples_ref.at[:, :, at], held.at[:, :, at], load_sem.at[c]
        )

    rest = pltpu.make_async_copy(
        samples_ref.at[:, :, pl.ds(chunks * per, TAIL)],
        held.at[:, :, pl.ds(chunks * per, TAIL)],
        load_sem.at[chunks],
    )
    for c in range(chunks):
        load(c).start()
    rest.start()

    spread[...] = jnp.zeros_like(spread)
    barrier = pltpu.get_barrier_semaphore()
    for k in order:
        pl.semaphore_signal(
            barrier, inc=1, device_id={"tile": partner(me, k, bits)}, device_id_type=MESH
        )

    def out_copy(c, k):
        there = partner(me, k, bits)
        return pltpu.make_async_remote_copy(
            src_ref=send.at[c, there],
            dst_ref=recv.at[c, me],
            send_sem=send_sem.at[c, k],
            recv_sem=recv_sem.at[c, k],
            device_id={"tile": there},
            device_id_type=MESH,
        )

    def own_copy(c):
        return pltpu.make_async_copy(send.at[c, me], recv.at[c, me], own_sem.at[c])

    tap_index = lax.broadcasted_iota(jnp.int32, (KEEP * 2, LANES), 1) & (NCHAN - 1)
    is_imag = lax.broadcasted_iota(jnp.int32, (KEEP * 2, LANES), 0) & 1 == 1
    angles = (tap_index * chan_ref[...] & (NCHAN - 1)).astype(jnp.float32) * (
        2.0 * math.pi / NCHAN
    )
    cosine = jnp.cos(angles) * (1.0 / math.sqrt(NCHAN))
    sine_part = jnp.sin(angles) * (1.0 / math.sqrt(NCHAN))
    table = [
        jnp.where(is_imag, -sine_part, cosine),
        jnp.where(is_imag, cosine, sine_part),
    ]
    table = [side.astype(jnp.bfloat16).astype(jnp.float32) for side in table]
    for dt in range(DT):
        for k in range(TAPS):
            at = (dt + k) * NCHAN
            spread[dt : dt + 1, at : at + NCHAN] = fir_ref[k : k + 1, :]
    for r in range(2):
        for b in range(WIDE // LANES):
            taps = spread[:, b * LANES : (b + 1) * LANES]
            both = table[r][:, None, :] * taps[None]
            filt[:, r * WIDE + b * LANES : r * WIDE + (b + 1) * LANES] = both.reshape(
                KEEP * 2 * DT, LANES
            ).astype(jnp.bfloat16)
    window[...] = jnp.zeros_like(window)
    pl.semaphore_wait(barrier, tiles - 1)
    load(0).wait()

    def channelize(c, carry):
        @pl.when(c + 1 < chunks)
        def _():
            load(c + 1).wait()

        @pl.when(c + 1 == chunks)
        def _():
            rest.wait()

        parts = []
        for f in range(2):
            for r in range(2):
                for q in range(8):
                    at = (c * 16 + f * 8 + q) * STRIDE
                    rows = slice(q * inputs, (q + 1) * inputs)
                    window[rows, r * WIDE : r * WIDE + STRIDE] = held[
                        r, :, pl.ds(pl.multiple_of(at, STRIDE), STRIDE)
                    ]
                    window[rows, r * WIDE + STRIDE : r * WIDE + STRIDE + TAIL] = held[
                        r, :, pl.ds(pl.multiple_of(at + STRIDE, STRIDE), TAIL)
                    ]
            got = lax.dot_general(
                filt[...], window[...], NT, preferred_element_type=jnp.float32
            )
            for h in range(2):
                parts.append(
                    got[:, h * LANES : (h + 1) * LANES].reshape(KEEP * 2, DT, LANES)
                )
        block = jnp.concatenate(parts, axis=1).astype(jnp.bfloat16)
        send[c] = block.reshape(tiles, chans * 2, 4 * DT, LANES)
        for k in order:
            out_copy(c, k).start()
        own_copy(c).start()
        return carry

    lax.fori_loop(0, chunks, channelize, 0)
    total[...] = jnp.zeros_like(total)

    def correlate(x, carry):
        for half in range(2):
            for k in order:
                out_copy(2 * x + half, k).wait_recv()
            own_copy(2 * x + half).wait()

        def turn(src, inner):
            rows = 4 * DT * 2
            for ch in range(chans):
                sides = []
                for p in range(2):
                    for half in range(2):
                        sides.append(recv[2 * x + half, src, ch * 2 + p])
                re0, re1, im0, im1 = sides
                one = jnp.concatenate([re0, re1, im0, im1], axis=0).T
                two = jnp.concatenate([-im0, -im1, re0, re1], axis=0).T
                place = pl.ds(pl.multiple_of(src * inputs, inputs), inputs)
                for g in range(LANES // inputs):
                    at = slice(g * 2 * rows, (g + 1) * 2 * rows)
                    left[ch, place, at] = one[g * inputs : (g + 1) * inputs]
                    right[ch, place, at] = two[g * inputs : (g + 1) * inputs]
            return inner

        lax.fori_loop(0, tiles, turn, 0)
        for ch in range(chans):
            for j in range(NBLK):
                cols = slice(j * BLOCK, (j + 1) * BLOCK)
                rhs = jnp.concatenate([left[ch, cols, :], right[ch, cols, :]], axis=0)
                got = lax.dot_general(
                    left[ch, : (j + 1) * BLOCK, :],
                    rhs,
                    NT,
                    preferred_element_type=jnp.float32,
                )
                for i in range(j + 1):
                    q = ch * NPAIR + i * NBLK - i * (i - 1) // 2 + j - i
                    for p in range(2):
                        total[q, p] += got[
                            i * BLOCK : (i + 1) * BLOCK, p * BLOCK : (p + 1) * BLOCK
                        ]
        return carry

    lax.fori_loop(0, chunks // 2, correlate, 0)

    scale = 1.0 / (chunks * 16 * DT)
    for p in range(NPAIR):
        q = layout_ref[p]
        for ch in range(chans):
            out_ref[ch * NPAIR + p] = total[ch * NPAIR + q] * scale

    def drain(c, carry):
        for k in order:
            out_copy(c, k).wait_send()
        return carry

    lax.fori_loop(0, chunks, drain, 0)


def fused(samples, fir_taps, chan_map, layout):
    tiles = lax.axis_size("tile")
    inputs = samples.shape[1]
    spec_count = samples.shape[2] // NCHAN - TAPS + 1
    chunks = spec_count // (16 * DT)
    chans = KEEP // tiles
    rows = jnp.repeat(chan_map, 2).reshape(KEEP * 2, 1)
    rows = jnp.broadcast_to(rows, (KEEP * 2, LANES))
    half = 4 * DT
    blocks = (chunks, tiles, chans * 2, half, LANES)
    turned = (chans, tiles * inputs, 4 * half * LANES // inputs)
    result = (chans * NPAIR, 2, BLOCK, BLOCK)
    vmem = pl.BlockSpec(memory_space=pltpu.VMEM)
    return pl.pallas_call(
        functools.partial(kernel, tiles, chunks),
        out_shape=jax.ShapeDtypeStruct(result, jnp.float32),
        in_specs=[
            pl.BlockSpec(memory_space=pltpu.SMEM),
            vmem,
            vmem,
            pl.BlockSpec(memory_space=pl.ANY),
        ],
        out_specs=vmem,
        scratch_shapes=[
            pltpu.VMEM(samples.shape, jnp.bfloat16),
            pltpu.VMEM((DT, WIDE), jnp.float32),
            pltpu.VMEM((KEEP * 2 * DT, 2 * WIDE), jnp.bfloat16),
            pltpu.VMEM((8 * inputs, 2 * WIDE), jnp.bfloat16),
            pltpu.VMEM(blocks, jnp.bfloat16),
            pltpu.VMEM(blocks, jnp.bfloat16),
            pltpu.VMEM(turned, jnp.bfloat16),
            pltpu.VMEM(turned, jnp.bfloat16),
            pltpu.VMEM(result, jnp.float32),
            pltpu.SemaphoreType.DMA((chunks + 1,)),
            pltpu.SemaphoreType.DMA((chunks,)),
            pltpu.SemaphoreType.DMA((chunks, tiles)),
            pltpu.SemaphoreType.DMA((chunks, tiles)),
        ],
        compiler_params=pltpu.CompilerParams(
            collective_id=0,
            has_side_effects=True,
            vmem_limit_bytes=48 * 1024 * 1024,
        ),
    )(layout, rows, fir_taps, samples)


def plain(samples, fir_taps, chan_map, layout):
    tiles = lax.axis_size("tile")
    inputs = samples.shape[1]
    spec_count = samples.shape[2] // NCHAN - TAPS + 1
    summed = jnp.zeros((2, inputs, spec_count * NCHAN), jnp.float32)
    for k in range(TAPS):
        part = lax.slice_in_dim(samples, k * NCHAN, (k + spec_count) * NCHAN, axis=2)
        summed = summed + part.astype(jnp.float32) * jnp.tile(fir_taps[k], spec_count)
    weighted = summed.astype(jnp.bfloat16).reshape(2, inputs, spec_count, NCHAN)
    spectra = jnp.einsum(
        "rnqc,ritn->ciqt", dft_table(chan_map), weighted, preferred_element_type=jnp.float32
    ).astype(jnp.bfloat16)
    rows = KEEP * NPAIR // tiles
    held = max(1, rows // NPAIR)
    spectra = jnp.repeat(spectra, max(1, NPAIR // rows), axis=0)
    spectra = spectra.reshape(tiles, held, inputs, 2, spec_count)
    got = lax.all_to_all(spectra, "tile", split_axis=0, concat_axis=2, tiled=True)
    got = got.reshape(held, tiles * inputs, 2, spec_count)
    swapped = jnp.stack([-got[:, :, 1], got[:, :, 0]], 2)
    first, second = pair_tables(NBLK)
    kinds = [
        jnp.einsum("capt,cbpt->cab", got, side, preferred_element_type=jnp.float32)
        for side in (got, swapped)
    ]
    blocks = jnp.stack(
        [
            jnp.stack(
                [
                    kind[:, i * BLOCK : (i + 1) * BLOCK, j * BLOCK : (j + 1) * BLOCK]
                    for kind in kinds
                ],
                1,
            )
            for i, j in zip(first, second)
        ],
        1,
    )
    start = lax.axis_index("tile") * rows % NPAIR
    out = []
    for row in range(rows):
        spot = (start + row) % NPAIR
        pair = jnp.sum(jnp.where(jnp.arange(NPAIR) == spot, layout, 0))
        chosen = (jnp.arange(NPAIR) == pair)[:, None, None, None]
        out.append(jnp.sum(jnp.where(chosen, blocks[row // NPAIR], 0.0), 0))
    return jnp.stack(out) / spec_count


def on_device(samples, fir_taps, chan_map, layout):
    tiles = lax.axis_size("tile")
    inputs = samples.shape[1]
    spec_count = samples.shape[2] // NCHAN - TAPS + 1
    fits = tiles == 16 and inputs == 32 and spec_count % (32 * DT) == 0
    return (fused if fits and spec_count <= 1024 else plain)(
        samples, fir_taps, chan_map, layout
    )


def solution(mesh):
    placed = (P(None, ("group", "tile"), None), P(), P(), P())
    return jax.shard_map(
        on_device,
        mesh=mesh,
        in_specs=placed,
        out_specs=P(("group", "tile"), None, None, None),
        check_vma=False,
    )
```

```python
import functools
import math

import jax
import jax.numpy as jnp
import numpy as np
from jax import lax
from jax.experimental import pallas as pl
from jax.experimental.pallas import tpu as pltpu
from jax.sharding import PartitionSpec as P

NCHAN = 64
KEEP = 32
TAPS = 8
BLOCK = 128
NBLK = 4
NPAIR = 10

DT = 8
STRIDE = DT * NCHAN
TAIL = (TAPS - 1) * NCHAN
WIDE = 2 * STRIDE
LANES = 128
MESH = pl.DeviceIdType.MESH
NT = (((1,), (1,)), ((), ()))


def pair_tables(block_count):
    pairs = [(i, j) for i in range(block_count) for j in range(i, block_count)]
    return tuple(np.array(side, np.int32) for side in zip(*pairs))


def dft_table(channels):
    tap_index = jnp.arange(NCHAN, dtype=jnp.int32)
    angles = (tap_index[:, None] * channels[None] % NCHAN).astype(jnp.float32) * (
        2.0 * math.pi / NCHAN
    )
    scaling = 1.0 / math.sqrt(NCHAN)
    cosine = jnp.cos(angles) * scaling
    sine_part = jnp.sin(angles) * scaling
    real_rows = jnp.stack([cosine, -sine_part], 1)
    imag_rows = jnp.stack([sine_part, cosine], 1)
    return jnp.stack([real_rows, imag_rows], 0).astype(jnp.bfloat16)


def partner(me, k, bits):
    return sum(
        ((me // (1 << b) + (k >> b & 1)) % 2) * (1 << b) for b in range(bits)
    )


def kernel(
    tiles,
    chunks,
    layout_ref,
    chan_ref,
    fir_ref,
    samples_ref,
    out_ref,
    held,
    spread,
    filt,
    window,
    send,
    recv,
    left,
    right,
    total,
    load_sem,
    own_sem,
    send_sem,
    recv_sem,
):
    bits = tiles.bit_length() - 1
    me = lax.axis_index("tile")
    per = 16 * STRIDE
    inputs = samples_ref.shape[1]
    order = list(range(1, tiles))
    chans = KEEP // tiles

    def load(c):
        at = pl.ds(pl.multiple_of(c * per, per), per)
        return pltpu.make_async_copy(
            samples_ref.at[:, :, at], held.at[:, :, at], load_sem.at[c]
        )

    rest = pltpu.make_async_copy(
        samples_ref.at[:, :, pl.ds(chunks * per, TAIL)],
        held.at[:, :, pl.ds(chunks * per, TAIL)],
        load_sem.at[chunks],
    )
    for c in range(chunks):
        load(c).start()
    rest.start()

    spread[...] = jnp.zeros_like(spread)
    barrier = pltpu.get_barrier_semaphore()
    for k in order:
        pl.semaphore_signal(
            barrier, inc=1, device_id={"tile": partner(me, k, bits)}, device_id_type=MESH
        )

    def out_copy(c, k):
        there = partner(me, k, bits)
        return pltpu.make_async_remote_copy(
            src_ref=send.at[c, there],
            dst_ref=recv.at[c, me],
            send_sem=send_sem.at[c, k],
            recv_sem=recv_sem.at[c, k],
            device_id={"tile": there},
            device_id_type=MESH,
        )

    def own_copy(c):
        return pltpu.make_async_copy(send.at[c, me], recv.at[c, me], own_sem.at[c])

    tap_index = lax.broadcasted_iota(jnp.int32, (KEEP * 2, LANES), 1) & (NCHAN - 1)
    is_imag = lax.broadcasted_iota(jnp.int32, (KEEP * 2, LANES), 0) & 1 == 1
    angles = (tap_index * chan_ref[...] & (NCHAN - 1)).astype(jnp.float32) * (
        2.0 * math.pi / NCHAN
    )
    cosine = jnp.cos(angles) * (1.0 / math.sqrt(NCHAN))
    sine_part = jnp.sin(angles) * (1.0 / math.sqrt(NCHAN))
    table = [
        jnp.where(is_imag, -sine_part, cosine),
        jnp.where(is_imag, cosine, sine_part),
    ]
    table = [side.astype(jnp.bfloat16).astype(jnp.float32) for side in table]
    for dt in range(DT):
        for k in range(TAPS):
            at = (dt + k) * NCHAN
            spread[dt : dt + 1, at : at + NCHAN] = fir_ref[k : k + 1, :]
    for r in range(2):
        for b in range(WIDE // LANES):
            taps = spread[:, b * LANES : (b + 1) * LANES]
            both = table[r][:, None, :] * taps[None]
            filt[:, r * WIDE + b * LANES : r * WIDE + (b + 1) * LANES] = both.reshape(
                KEEP * 2 * DT, LANES
            ).astype(jnp.bfloat16)
    window[...] = jnp.zeros_like(window)
    pl.semaphore_wait(barrier, tiles - 1)
    load(0).wait()

    def channelize(c, carry):
        @pl.when(c + 1 < chunks)
        def _():
            load(c + 1).wait()

        @pl.when(c + 1 == chunks)
        def _():
            rest.wait()

        parts = []
        for f in range(2):
            for r in range(2):
                for q in range(8):
                    at = (c * 16 + f * 8 + q) * STRIDE
                    rows = slice(q * inputs, (q + 1) * inputs)
                    window[rows, r * WIDE : r * WIDE + STRIDE] = held[
                        r, :, pl.ds(pl.multiple_of(at, STRIDE), STRIDE)
                    ]
                    window[rows, r * WIDE + STRIDE : r * WIDE + STRIDE + TAIL] = held[
                        r, :, pl.ds(pl.multiple_of(at + STRIDE, STRIDE), TAIL)
                    ]
            got = lax.dot_general(
                filt[...], window[...], NT, preferred_element_type=jnp.float32
            )
            for h in range(2):
                parts.append(
                    got[:, h * LANES : (h + 1) * LANES].reshape(KEEP * 2, DT, LANES)
                )
        block = jnp.concatenate(parts, axis=1).astype(jnp.bfloat16)
        send[c] = block.reshape(tiles, chans * 2, 4 * DT, LANES)
        for k in order:
            out_copy(c, k).start()
        own_copy(c).start()
        return carry

    lax.fori_loop(0, chunks, channelize, 0)
    total[...] = jnp.zeros_like(total)

    def correlate(x, carry):
        for half in range(2):
            for k in order:
                out_copy(2 * x + half, k).wait_recv()
            own_copy(2 * x + half).wait()

        def turn(src, inner):
            rows = 4 * DT * 2
            for ch in range(chans):
                sides = []
                for p in range(2):
                    for half in range(2):
                        sides.append(recv[2 * x + half, src, ch * 2 + p])
                re0, re1, im0, im1 = sides
                one = jnp.concatenate([re0, re1, im0, im1], axis=0).T
                two = jnp.concatenate([-im0, -im1, re0, re1], axis=0).T
                place = pl.ds(pl.multiple_of(src * inputs, inputs), inputs)
                for g in range(LANES // inputs):
                    at = slice(g * 2 * rows, (g + 1) * 2 * rows)
                    left[ch, place, at] = one[g * inputs : (g + 1) * inputs]
                    right[ch, place, at] = two[g * inputs : (g + 1) * inputs]
            return inner

        lax.fori_loop(0, tiles, turn, 0, unroll=4)
        for ch in range(chans):
            for j in range(NBLK):
                cols = slice(j * BLOCK, (j + 1) * BLOCK)
                rhs = jnp.concatenate([left[ch, cols, :], right[ch, cols, :]], axis=0)
                got = lax.dot_general(
                    left[ch, : (j + 1) * BLOCK, :],
                    rhs,
                    NT,
                    preferred_element_type=jnp.float32,
                )
                for i in range(j + 1):
                    q = ch * NPAIR + i * NBLK - i * (i - 1) // 2 + j - i
                    for p in range(2):
                        total[q, p] += got[
                            i * BLOCK : (i + 1) * BLOCK, p * BLOCK : (p + 1) * BLOCK
                        ]
        return carry

    lax.fori_loop(0, chunks // 2, correlate, 0)

    scale = 1.0 / (chunks * 16 * DT)
    for p in range(NPAIR):
        q = layout_ref[p]
        for ch in range(chans):
            out_ref[ch * NPAIR + p] = total[ch * NPAIR + q] * scale

    def drain(c, carry):
        for k in order:
            out_copy(c, k).wait_send()
        return carry

    lax.fori_loop(0, chunks, drain, 0)


def fused(samples, fir_taps, chan_map, layout):
    tiles = lax.axis_size("tile")
    inputs = samples.shape[1]
    spec_count = samples.shape[2] // NCHAN - TAPS + 1
    chunks = spec_count // (16 * DT)
    chans = KEEP // tiles
    rows = jnp.repeat(chan_map, 2).reshape(KEEP * 2, 1)
    rows = jnp.broadcast_to(rows, (KEEP * 2, LANES))
    half = 4 * DT
    blocks = (chunks, tiles, chans * 2, half, LANES)
    turned = (chans, tiles * inputs, 4 * half * LANES // inputs)
    result = (chans * NPAIR, 2, BLOCK, BLOCK)
    vmem = pl.BlockSpec(memory_space=pltpu.VMEM)
    return pl.pallas_call(
        functools.partial(kernel, tiles, chunks),
        out_shape=jax.ShapeDtypeStruct(result, jnp.float32),
        in_specs=[
            pl.BlockSpec(memory_space=pltpu.SMEM),
            vmem,
            vmem,
            pl.BlockSpec(memory_space=pl.ANY),
        ],
        out_specs=vmem,
        scratch_shapes=[
            pltpu.VMEM(samples.shape, jnp.bfloat16),
            pltpu.VMEM((DT, WIDE), jnp.float32),
            pltpu.VMEM((KEEP * 2 * DT, 2 * WIDE), jnp.bfloat16),
            pltpu.VMEM((8 * inputs, 2 * WIDE), jnp.bfloat16),
            pltpu.VMEM(blocks, jnp.bfloat16),
            pltpu.VMEM(blocks, jnp.bfloat16),
            pltpu.VMEM(turned, jnp.bfloat16),
            pltpu.VMEM(turned, jnp.bfloat16),
            pltpu.VMEM(result, jnp.float32),
            pltpu.SemaphoreType.DMA((chunks + 1,)),
            pltpu.SemaphoreType.DMA((chunks,)),
            pltpu.SemaphoreType.DMA((chunks, tiles)),
            pltpu.SemaphoreType.DMA((chunks, tiles)),
        ],
        compiler_params=pltpu.CompilerParams(
            collective_id=0,
            has_side_effects=True,
            vmem_limit_bytes=48 * 1024 * 1024,
        ),
    )(layout, rows, fir_taps, samples)


def plain(samples, fir_taps, chan_map, layout):
    tiles = lax.axis_size("tile")
    inputs = samples.shape[1]
    spec_count = samples.shape[2] // NCHAN - TAPS + 1
    summed = jnp.zeros((2, inputs, spec_count * NCHAN), jnp.float32)
    for k in range(TAPS):
        part = lax.slice_in_dim(samples, k * NCHAN, (k + spec_count) * NCHAN, axis=2)
        summed = summed + part.astype(jnp.float32) * jnp.tile(fir_taps[k], spec_count)
    weighted = summed.astype(jnp.bfloat16).reshape(2, inputs, spec_count, NCHAN)
    spectra = jnp.einsum(
        "rnqc,ritn->ciqt", dft_table(chan_map), weighted, preferred_element_type=jnp.float32
    ).astype(jnp.bfloat16)
    rows = KEEP * NPAIR // tiles
    held = max(1, rows // NPAIR)
    spectra = jnp.repeat(spectra, max(1, NPAIR // rows), axis=0)
    spectra = spectra.reshape(tiles, held, inputs, 2, spec_count)
    got = lax.all_to_all(spectra, "tile", split_axis=0, concat_axis=2, tiled=True)
    got = got.reshape(held, tiles * inputs, 2, spec_count)
    swapped = jnp.stack([-got[:, :, 1], got[:, :, 0]], 2)
    first, second = pair_tables(NBLK)
    kinds = [
        jnp.einsum("capt,cbpt->cab", got, side, preferred_element_type=jnp.float32)
        for side in (got, swapped)
    ]
    blocks = jnp.stack(
        [
            jnp.stack(
                [
                    kind[:, i * BLOCK : (i + 1) * BLOCK, j * BLOCK : (j + 1) * BLOCK]
                    for kind in kinds
                ],
                1,
            )
            for i, j in zip(first, second)
        ],
        1,
    )
    start = lax.axis_index("tile") * rows % NPAIR
    out = []
    for row in range(rows):
        spot = (start + row) % NPAIR
        pair = jnp.sum(jnp.where(jnp.arange(NPAIR) == spot, layout, 0))
        chosen = (jnp.arange(NPAIR) == pair)[:, None, None, None]
        out.append(jnp.sum(jnp.where(chosen, blocks[row // NPAIR], 0.0), 0))
    return jnp.stack(out) / spec_count


def on_device(samples, fir_taps, chan_map, layout):
    tiles = lax.axis_size("tile")
    inputs = samples.shape[1]
    spec_count = samples.shape[2] // NCHAN - TAPS + 1
    fits = tiles == 16 and inputs == 32 and spec_count % (32 * DT) == 0
    return (fused if fits and spec_count <= 1024 else plain)(
        samples, fir_taps, chan_map, layout
    )


def solution(mesh):
    placed = (P(None, ("group", "tile"), None), P(), P(), P())
    return jax.shard_map(
        on_device,
        mesh=mesh,
        in_specs=placed,
        out_specs=P(("group", "tile"), None, None, None),
        check_vma=False,
    )
```
